128 devices in a mesh: replica: 2 (over z_lo), fsdp: 4 (over y), mp: 16 (over x, z_hi, core).
Axes of the slice: x: 4, y: 4, z: 4 (z_hi: 2, z_lo: 2; z = z_hi * 2 + z_lo), core: 2. Of those that a mesh axis runs over, the one named last changes fastest.
Arguments:
- inputs: bfloat16 [8, 2048, 1024], P(('replica', 'fsdp'), 'mp'), may hold values from -6 to 6
- w_qkv: bfloat16 [1, 1024, 3, 1024], P(None, 'fsdp', None, 'mp'), may hold values from -0.1875 to 0.1875
- b_qv: bfloat16 [1, 2, 1024], P(None, None, 'mp'), may hold values from -1.5 to 1.5
- w_out: bfloat16 [1, 1024, 1024], P(None, 'mp', 'fsdp'), may hold values from -1.5 to 1.5
- w_in: bfloat16 [1, 1024, 4096], P(None, 'fsdp', 'mp'), may hold values from -0.1875 to 0.1875
- b_in: bfloat16 [1, 4096], P(None, 'mp'), may hold values from -2.5 to 2.5
- down_weight: bfloat16 [1, 4096, 1024], P(None, 'mp', 'fsdp'), may hold values from -0.125 to 0.125
- norm_gains: bfloat16 [1, 2, 1024], replicated, may hold values from 0.5 to 1.5
- shifts: bfloat16 [1, 4, 1024], replicated, may hold values from -1.5 to 1.5
- bias_table: bfloat16 [1, 32, 16], P(None, None, 'mp'), may hold values from -4 to 4
- buckets: int32 [8, 4095], P(('replica', 'fsdp')), may hold values from 0 to 31
- cotangent: bfloat16 [8, 2048, 1024], P(('replica', 'fsdp'), 'mp'), may hold values from -6 to 6
Outputs:
- outputs: bfloat16 [8, 2048, 1024], P(('replica', 'fsdp'), 'mp')
- grad_inputs: float32 [8, 2048, 1024], P(('replica', 'fsdp'), 'mp')
- grad_w_qkv: float32 [1, 1024, 3, 1024], P(None, 'fsdp', None, 'mp')
- grad_b_qv: float32 [1, 2, 1024], P(None, None, 'mp')
- grad_w_out: float32 [1, 1024, 1024], P(None, 'mp', 'fsdp')
- grad_w_in: float32 [1, 1024, 4096], P(None, 'fsdp', 'mp')
- grad_b_in: float32 [1, 4096], P(None, 'mp')
- grad_w_back: float32 [1, 4096, 1024], P(None, 'mp', 'fsdp')
- grad_gains: float32 [1, 2, 1024], replicated
- grad_shifts: float32 [1, 4, 1024], replicated
- grad_table: float32 [1, 32, 16], P(None, None, 'mp')
The draws below stay inside these ranges and needn't reach their ends.
All inputs are finite; a program needn't handle non-finite values.
Results may differ from the reference program's by a relative error of at most 0.022.
Values may be sent and summed in bfloat16 or wider, within the bound.
A program may use at most 128 MiB of HBM per device.

```python
import jax
import jax.numpy as jnp
from jax import lax

D = 1024
HEADS = 16
HEAD_DIM = 64
FF = 4096
BUCKETS = 32
NL = 1
L = 2048
SEQS = 8


def touch_ends(values, stream_key, smallest, high):
    dims = values.shape
    index_at = [jax.random.randint(jax.random.fold_in(stream_key, axis), (), 0, dims[axis]) for axis in range(len(dims))]
    values = values.at[tuple(index_at)].set(smallest)
    longest = dims.index(max(dims))
    index_at[longest] = (index_at[longest] + 1) % dims[longest]
    return values.at[tuple(index_at)].set(high)


def block_levels(rng, dims, pieces, low, high):
    loudness, own = 1.0, jax.random.fold_in(rng, 6)
    for position, blocks in pieces:
        draws = jnp.exp(jax.random.uniform(jax.random.fold_in(own, position), (blocks,), jnp.float32, low / len(pieces), high / len(pieces)))
        loudness = loudness * jnp.repeat(draws, dims[position] // blocks).reshape([-1 if axis == position else 1 for axis in range(len(dims))])
    return loudness


def gaussian(key, extent, deviation, limit, pieces=(), kind=jnp.bfloat16):
    drawn = deviation * jax.random.normal(key, extent, jnp.float32)
    if pieces:
        drawn = drawn * block_levels(key, extent, pieces, -0.22, 0.18)
    return jnp.clip(drawn, -limit, limit).astype(kind)


def setup_inputs(seed: int = 0) -> dict:
    streams_of = jax.random.split(jax.random.key(seed), 13)
    return {
        "inputs": gaussian(streams_of[0], (SEQS, L, D), 1.0, 6.0, ((0, 8), (1, 16))),
        "w_qkv": gaussian(streams_of[1], (NL, D, 3, D), D ** -0.5, 0.1875, ((1, 4), (3, 16))),
        "b_qv": gaussian(streams_of[2], (NL, 2, D), 0.3, 1.5, ((2, 16),)),
        "w_out": gaussian(streams_of[3], (NL, D, D), (D // 64) ** -0.5, 1.5, ((1, 16), (2, 4))),
        "w_in": gaussian(streams_of[4], (NL, D, FF), D ** -0.5, 0.1875, ((1, 4), (2, 16))),
        "b_in": gaussian(streams_of[5], (NL, FF), 0.5, 2.5, ((1, 16),)),
        "down_weight": gaussian(streams_of[6], (NL, FF, D), (FF // 2) ** -0.5, 0.125, ((1, 16), (2, 4))),
        "norm_gains": jnp.clip(1.0 + 0.1 * jax.random.normal(streams_of[7], (NL, 2, D), jnp.float32), 0.5, 1.5).astype(jnp.bfloat16),
        "shifts": gaussian(streams_of[8], (NL, 4, D), 0.3, 1.5),
        "bias_table": gaussian(streams_of[9], (NL, BUCKETS, HEADS), 1.0, 4.0, ((2, 16),)),
        "buckets": touch_ends(jax.random.randint(streams_of[10], (SEQS, 2 * L - 1), 0, BUCKETS), jax.random.fold_in(streams_of[10], 1), 0, BUCKETS - 1).astype(jnp.int32),
        "cotangent": gaussian(streams_of[11], (SEQS, L, D), 1.0, 6.0, ((0, 8), (1, 16))),
    }


@jax.custom_vjp
def low(v):
    return lax.optimization_barrier(v.astype(jnp.bfloat16)).astype(jnp.float32)

@jax.custom_vjp
def low_back(v):
    return v

def low_keep(v):
    return (low(v), None)

def low_pass(kept, grad):
    return (grad,)

def back_keep(v):
    return (v, None)

def back_low(kept, grad):
    return (low(grad),)
low.defvjp(low_keep, low_pass)
low_back.defvjp(back_keep, back_low)
EPSILON = 1e-05
PRECISE = lax.Precision.HIGHEST

def matmul(operand, matrix):
    return jnp.dot(operand, matrix, precision=PRECISE, preferred_element_type=jnp.float32)

def layer_norm(values, gain_vec, shift_vec):
    center = values - lax.optimization_barrier(jnp.mean(values, axis=-1, keepdims=True))
    variance = lax.optimization_barrier(jnp.mean(center * center, axis=-1, keepdims=True))
    return center * lax.rsqrt(variance + EPSILON) * gain_vec + shift_vec

def score_bias(table_now, bucket_row):
    relative = table_now[bucket_row]
    offset = jnp.arange(L, dtype=jnp.int32)[None, :] - jnp.arange(L, dtype=jnp.int32)[:, None] + (L - 1)
    return jnp.transpose(relative[offset], (2, 0, 1))

def one_layer(hidden, layer_weights, bucket_row):
    w_qkv, b_qv, w_out, w_in, b_in, down_weight, gain_pair, shift_rows, table_now = layer_weights
    rounded = low(hidden)
    bundled_weight = jnp.einsum('ld,dkc->lkc', rounded, w_qkv, precision=PRECISE)
    head_shape = (L, HEADS, HEAD_DIM)
    query = low(low_back(bundled_weight[:, 0] + b_qv[0])).reshape(head_shape)
    key_heads = low(low_back(bundled_weight[:, 1])).reshape(head_shape)
    head_values = low(low_back(bundled_weight[:, 2] + b_qv[1])).reshape(head_shape)
    scores = jnp.einsum('qhd,khd->hqk', query, key_heads, precision=PRECISE) * float(HEAD_DIM) ** (-0.5)
    scores = low_back(scores + score_bias(table_now, bucket_row))
    attention_probs = low(jax.nn.softmax(scores, axis=-1))
    context = jnp.einsum('hqk,khd->qhd', attention_probs, head_values, precision=PRECISE).reshape(L, D)
    context = low(low_back(context))
    attended = low_back(matmul(context, w_out) + shift_rows[0])
    after_attn = layer_norm(hidden + attended, gain_pair[0], shift_rows[1])
    middle = low_back(matmul(low(after_attn), w_in) + b_in)
    activated = low(jax.nn.gelu(middle, approximate=False))
    mlp_out = low_back(matmul(activated, down_weight) + shift_rows[2])
    return layer_norm(after_attn + mlp_out, gain_pair[1], shift_rows[3])

def forward(sequence, layer_weights, bucket_row):
    hidden = sequence
    for layer_at in range(NL):
        hidden = one_layer(hidden, tuple((stacked[layer_at] for stacked in layer_weights)), bucket_row)
    return hidden

def reference(inputs, w_qkv, b_qv, w_out, w_in, b_in, down_weight, norm_gains, shifts, bias_table, buckets, cotangent):
    layer_weights = tuple((weight.astype(jnp.float32) for weight in (w_qkv, b_qv, w_out, w_in, b_in, down_weight, norm_gains, shifts, bias_table)))

    def per_sequence(totals, scanned):
        sequence, bucket_row, upstream = scanned

        def closed(sequence_in, params_in):
            return forward(sequence_in, params_in, bucket_row)
        result, pullback = jax.vjp(closed, sequence.astype(jnp.float32), layer_weights)
        grad_sequence, grad_params = pullback(upstream.astype(jnp.float32))
        return (jax.tree.map(jnp.add, totals, grad_params), (result.astype(jnp.bfloat16), grad_sequence))
    initial = jax.tree.map(jnp.zeros_like, layer_weights)
    totals, (outputs, grad_inputs) = lax.scan(per_sequence, initial, (inputs, buckets, cotangent))
    return (outputs, grad_inputs, totals[0], totals[1], totals[2], totals[3], totals[4], totals[5], totals[6], totals[7], totals[8])
```

```python
import functools

import jax
import jax.numpy as jnp
from jax import lax
from jax.experimental import pallas as pl
from jax.experimental.pallas import tpu as pltpu
from jax.sharding import PartitionSpec as P

D = 1024
HEAD_DIM = 64
BUCKETS = 32
EPSILON = 1e-05
LENGTH = 2048
STRIP = 256
BAND = 4096
WQ_ROWS = 272
WR_ROWS = 592
GRAD_ROWS = 832
VMEM = pltpu.VMEM
BF16 = jnp.bfloat16
F32 = jnp.float32
MESH = pl.DeviceIdType.MESH
SEMS = pltpu.SemaphoreType.DMA


class Place:
    def __init__(self):
        rep, row, mp = (lax.axis_index(a) for a in ("replica", "fsdp", "mp"))
        self.rep, self.y = rep, row
        self.x, self.z, self.c = mp // 4, (mp // 2) % 2, mp % 2
        self.xr, self.xl, self.xo = (self.x + 1) % 4, (self.x + 3) % 4, (self.x + 2) % 4
        self.yr, self.yl, self.yo = (row + 1) % 4, (row + 3) % 4, (row + 2) % 4

        def at(rep=rep, y=row, x=self.x, z=self.z, c=self.c):
            return (rep, y, x * 4 + z * 2 + c)

        self.core = at(c=1 - self.c)
        self.half = at(z=1 - self.z)
        self.right, self.left = at(x=self.xr), at(x=self.xl)
        self.up, self.down = at(y=self.yr), at(y=self.yl)
        self.twin = at(rep=1 - rep)
        self.cross = at(rep=1 - rep, z=1 - self.z)


def greet(partners):
    barrier = pltpu.get_barrier_semaphore()
    for partner in partners:
        pl.semaphore_signal(barrier, inc=1, device_id=partner, device_id_type=MESH)
    pl.semaphore_wait(barrier, len(partners))


def remote(src, dst, sems, index, partner):
    return pltpu.make_async_remote_copy(
        src_ref=src,
        dst_ref=dst,
        send_sem=sems.at[0, index],
        recv_sem=sems.at[1, index],
        device_id=partner,
        device_id_type=MESH,
    )


def dot(a, b):
    return lax.dot_general(a, b, (((1,), (0,)), ((), ())), preferred_element_type=F32)


def dot_nt(a, b):
    return lax.dot_general(a, b, (((1,), (1,)), ((), ())), preferred_element_type=F32)


def dot_tn(a, b):
    return lax.dot_general(a, b, (((0,), (0,)), ((), ())), preferred_element_type=F32)


def gather_tokens(at, buf, sems, process):
    first, second, whole = pl.ds(0, 64), pl.ds(64, 64), pl.ds(0, 128)

    def copy(index, x, rows, partner):
        ref = buf.at[x, at.c, rows]
        return remote(ref, ref, sems, index, partner)

    c0 = copy(0, at.x, whole, at.core)
    a1, a2 = copy(1, at.x, first, at.right), copy(2, at.x, second, at.right)
    b1, b2 = copy(3, at.x, second, at.left), copy(4, at.x, first, at.left)
    f5, f6 = copy(5, at.xl, first, at.right), copy(6, at.xr, second, at.left)
    c7, c8 = copy(7, at.xl, whole, at.core), copy(8, at.xr, whole, at.core)
    c9 = copy(9, at.xo, whole, at.core)
    for each in (a1, b1, a2, b2, c0):
        each.start()
    c0.wait_recv()
    process(at.x)
    a1.wait_recv()
    f5.start()
    b1.wait_recv()
    f6.start()
    a2.wait_recv()
    c7.start()
    b2.wait_recv()
    c8.start()
    c7.wait_recv()
    process(at.xl)
    c8.wait_recv()
    process(at.xr)
    f5.wait_recv()
    f6.wait_recv()
    c9.start()
    c9.wait_recv()
    process(at.xo)
    for each in (c0, a1, a2, b1, b2, f5, f6, c7, c8, c9):
        each.wait_send()


def reduce_tokens(at, produce, parts, sc, rc, sx, rx, fx, sems, between=None):
    first, second = pl.ds(0, 64), pl.ds(64, 64)
    cores = []

    def make(j, x):
        produce(x, parts.at[j])
        sc[j] = parts[j, 1 - at.c].astype(BF16)
        cores.append(remote(sc.at[j], rc.at[j], sems, j, at.core))
        cores[j].start()

    make(0, at.xo)
    make(1, at.xr)
    cores[0].wait_recv()
    sx[0] = (parts[0, at.c] + rc[0].astype(F32)).astype(BF16)
    oa = remote(sx.at[0, first], rx.at[0], sems, 4, at.right)
    ob = remote(sx.at[0, second], rx.at[1], sems, 5, at.left)
    oa.start()
    ob.start()
    make(2, at.xl)
    cores[1].wait_recv()
    sx[1, second] = (parts[1, at.c, second] + rc[1, second].astype(F32)).astype(BF16)
    rb = remote(sx.at[1, second], fx.at[0, second], sems, 6, at.right)
    rb.start()
    cores[2].wait_recv()
    sx[2, first] = (parts[2, at.c, first] + rc[2, first].astype(F32)).astype(BF16)
    la = remote(sx.at[2, first], fx.at[1, first], sems, 7, at.left)
    la.start()
    make(3, at.x)
    oa.wait_recv()
    sx[1, first] = (parts[1, at.c, first] + rc[1, first].astype(F32) + rx[0].astype(F32)).astype(BF16)
    ra = remote(sx.at[1, first], fx.at[0, first], sems, 8, at.right)
    ra.start()
    ob.wait_recv()
    sx[2, second] = (
        parts[2, at.c, second] + rc[2, second].astype(F32) + rx[1].astype(F32)
    ).astype(BF16)
    lb = remote(sx.at[2, second], fx.at[1, second], sems, 9, at.left)
    lb.start()
    if between is not None:
        between()
    cores[3].wait_recv()
    for each in (rb, la, ra, lb):
        each.wait_recv()
    total = parts[3, at.c] + rc[3].astype(F32) + fx[0].astype(F32) + fx[1].astype(F32)
    for each in cores + [oa, ob, rb, la, ra, lb]:
        each.wait_send()
    return total


REDUCE_SCRATCH = [
    VMEM((4, 128, D), BF16),
    VMEM((4, 128, D), BF16),
    VMEM((3, 128, D), BF16),
    VMEM((2, 64, D), BF16),
    VMEM((2, 128, D), BF16),
]


class GatherRows:
    def __init__(self, at, buf, sems, rows):
        split = rows // 32 * 16
        first, second = pl.ds(0, split), pl.ds(split, rows - split)

        def copy(index, half, y, rows_, partner):
            ref = buf.at[half, y, rows_]
            return remote(ref, ref, sems, index, partner)

        whole = pl.ds(0, rows)
        self.cross = remote(buf.at[0, at.y, whole], buf.at[1, at.y, whole], sems, 0, at.cross)
        self.sets = []
        for h in range(2):
            b = 1 + 6 * h
            self.sets.append(
                (
                    copy(b, h, at.y, first, at.up),
                    copy(b + 1, h, at.y, second, at.down),
                    copy(b + 2, h, at.y, second, at.up),
                    copy(b + 3, h, at.y, first, at.down),
                    copy(b + 4, h, at.yl, first, at.up),
                    copy(b + 5, h, at.yr, second, at.down),
                )
            )

    def step0(self):
        self.cross.start()
        for each in self.sets[0][:4]:
            each.start()

    def step1(self):
        self.cross.wait_recv()
        for each in self.sets[1][:4]:
            each.start()

    def forward(self, h):
        s = self.sets[h]
        s[0].wait_recv()
        s[4].start()
        s[1].wait_recv()
        s[5].start()

    def finish(self):
        for s in self.sets:
            for each in s[2:]:
                each.wait_recv()
        self.cross.wait_send()
        for s in self.sets:
            for each in s:
                each.wait_send()


def project_kernel(x_ref, wq_own, wr_own, xg, wq, wr, packed, stage, xs, qs, rs, zs):
    at = Place()
    greet([at.core, at.half, at.cross, at.right, at.left, at.up, at.down])
    xg[at.x, at.c] = x_ref[...]
    wq[0, at.y] = wq_own[...]
    wr[0, at.y] = wr_own[...]
    gq = GatherRows(at, wq, qs, WQ_ROWS)
    gr = GatherRows(at, wr, rs, WR_ROWS)
    gq.step0()
    gr.step0()
    gq.step1()
    gq.forward(0)
    gq.forward(1)
    gq.finish()
    sends = []

    def process(x):
        rows = xg[x].reshape(256, D)
        j = len(sends)
        for h in range(2):
            weight = wq[h, :, 0:256, :].reshape(D, 256)
            bias = wq[h, at.y, 256:272, :].astype(F32)[0:1]
            out = (dot(rows, weight) + bias).astype(BF16)
            for t in range(3):
                part = out[:, 64 * t : 64 * t + 64]
                pair = jnp.concatenate([part[:128], part[128:]], axis=1)
                if h == 0:
                    packed[x * 2 + at.z, t] = pair
                else:
                    stage[j, t] = pair
        send = remote(stage.at[j], packed.at[x * 2 + at.z], zs, j, at.half)
        send.start()
        sends.append(send)

    gather_tokens(at, xg, xs, process)
    for send in sends:
        send.wait()
    gr.step1()
    gr.forward(0)
    gr.forward(1)
    gr.finish()


def unpack(pair):
    return jnp.concatenate([pair[:, :64], pair[:, 64:]], axis=0)


def pack(rows):
    return jnp.concatenate([rows[:128], rows[128:]], axis=1)


def attend_kernel(packed, seed, probs, context, context_packed, band, keys, values):
    step = pl.program_id(0)

    @pl.when(step == 0)
    def _():
        band[0:8] = seed[...]
        size = 8
        while size < STRIP:
            band[size : 2 * size] = pltpu.roll(band[0:size], size, 1)
            size *= 2
        for i in range(8):
            keys[256 * i : 256 * i + 256] = unpack(packed[i, 1])
            values[256 * i : 256 * i + 256] = unpack(packed[i, 2])

    query = unpack(packed[step, 0]) * jnp.asarray(0.125, BF16)
    offset = pl.multiple_of((7 - step) * STRIP, STRIP)
    scores = dot_nt(query, keys[...]) + band[:, pl.ds(offset, LENGTH)]
    peak = jnp.max(scores, axis=1, keepdims=True)
    powers = jnp.exp(scores - peak)
    total = jnp.sum(powers, axis=1, keepdims=True)
    prob = (powers * (1.0 / total)).astype(BF16)
    probs[...] = prob
    out = dot(prob, values[...])
    context[...] = out
    context_packed[0] = pack(out.astype(BF16))


def attend_back_kernel(
    packed, probs, context, grad_packed, out_packed, fold, sums,
    band, keys, values, grad_keys, grad_values, grad_query,
):
    step = pl.program_id(0)

    @pl.when(step == 0)
    def _():
        band[...] = jnp.zeros_like(band)
        grad_keys[...] = jnp.zeros_like(grad_keys)
        grad_values[...] = jnp.zeros_like(grad_values)
        for i in range(8):
            keys[256 * i : 256 * i + 256] = unpack(packed[i, 1])
            values[256 * i : 256 * i + 256] = unpack(packed[i, 2])

    query = unpack(packed[step, 0]) * jnp.asarray(0.125, BF16)
    upstream = unpack(grad_packed[step])
    prob = probs[...]
    dots = jnp.sum(upstream.astype(F32) * context[...], axis=1, keepdims=True)
    grad_scores = prob.astype(F32) * (dot_nt(upstream, values[...]) - dots)
    offset = pl.multiple_of((7 - step) * STRIP, STRIP)
    band[:, pl.ds(offset, LENGTH)] += grad_scores
    low = grad_scores.astype(BF16)
    gq = (dot(low, keys[...]) * 0.125).astype(BF16)
    grad_query[step] = gq
    out_packed[step, 0] = pack(gq)
    grad_keys[...] += dot(query.T, low)
    grad_values[...] += dot(upstream.T, prob)

    @pl.when(step == 7)
    def _():
        size = STRIP // 2
        while size >= 8:
            band[0:size] = band[0:size] + pltpu.roll(band[size : 2 * size], BAND - size, 1)
            size //= 2
        fold[...] = band[0:8]
        total_q = jnp.zeros((1, 64), F32)
        total_v = jnp.zeros((1, 64), F32)
        for i in range(8):
            total_q += jnp.sum(grad_query[i].astype(F32), axis=0, keepdims=True)
            cols = slice(256 * i, 256 * i + 256)
            out_packed[i, 1] = pack(grad_keys[:, cols].T.astype(BF16))
            gv = grad_values[:, cols].T.astype(BF16)
            total_v += jnp.sum(gv.astype(F32), axis=0, keepdims=True)
            out_packed[i, 2] = pack(gv)
        sums[0:1] = jnp.concatenate([total_q, total_v], axis=1)
        sums[1:8] = jnp.zeros((7, 128), F32)


def norm(values):
    center = values - jnp.mean(values, axis=-1, keepdims=True)
    inverse = lax.rsqrt(jnp.mean(center * center, axis=-1, keepdims=True) + EPSILON)
    return center * inverse, inverse


def norm_back(upstream, normed, inverse, gain):
    scaled = upstream * gain
    return inverse * (
        scaled
        - jnp.mean(scaled, axis=-1, keepdims=True)
        - normed * jnp.mean(scaled * normed, axis=-1, keepdims=True)
    )


def middle_kernel(
    ctx, x_ref, cot, wr, vectors,
    y_out, dz1_out, dctx_out, grads, small, grad_hidden,
    ctx_in, c2, hg, mg, ag, act, slope, gmid, parts,
    sc1, rc1, sx1, rx1, fx1, sc2, rc2, sx2, rx2, fx2, sc3, rc3, sx3, rx3, fx3,
    normed_ref, dz2_ref, dstage,
    zs, s1, s2, s3, s4, s5, s6, ds,
):
    at = Place()
    greet([at.core, at.half, at.right, at.left])
    swaps = []
    for j, x in enumerate((at.xo, at.xr, at.xl, at.x)):
        send = remote(ctx.at[x * 2 + 1 - at.z], ctx_in.at[x], zs, j, at.half)
        send.start()
        swaps.append(send)
    waiting = list(swaps)

    def out_partial(x, ref):
        waiting.pop(0).wait_recv()
        own, other = ctx[x * 2 + at.z], ctx_in[x]
        c2[x, 0] = jnp.concatenate([own[:, :64], other[:, :64]], axis=1)
        c2[x, 1] = jnp.concatenate([own[:, 64:], other[:, 64:]], axis=1)
        rows = c2[x].reshape(256, 128)
        for y in range(4):
            weight = wr[:, y, 512:576, :].reshape(128, 256)
            ref[:, :, 256 * y : 256 * y + 256] = dot(rows, weight).reshape(2, 128, 256)

    attended = reduce_tokens(at, out_partial, parts, sc1, rc1, sx1, rx1, fx1, s1)
    vec = vectors[...]
    gain1, gain2 = vec[0:1], vec[1:2]
    normed1, inverse1 = norm(x_ref[...].astype(F32) + (attended + vec[2:3]))
    normed_ref[...] = normed1
    after = normed1 * gain1 + vec[3:4]
    hg[at.x, at.c] = after.astype(BF16)

    def mlp_up(x):
        rows = hg[x].reshape(256, D)
        for h in range(2):
            weight = wr[h, :, 0:256, :].reshape(D, 256)
            bias = wr[h, at.y, 576:592, :].astype(F32)[0:1]
            u = dot(rows, weight) + bias
            phi = 0.5 * (1.0 + lax.erf(u * 0.7071067811865476))
            act[x, h] = (u * phi).astype(BF16)
            slope[x, h] = phi + u * (jnp.exp(-0.5 * u * u) * 0.3989422804014327)

    gather_tokens(at, hg, s2, mlp_up)

    def mlp_down(x, ref):
        for y in range(4):
            part = dot(act[x, 0], wr[0, y, 256:512, :]) + dot(act[x, 1], wr[1, y, 256:512, :])
            ref[:, :, 256 * y : 256 * y + 256] = part.reshape(2, 128, 256)

    mlp = reduce_tokens(at, mlp_down, parts, sc2, rc2, sx2, rx2, fx2, s3)
    normed1 = normed_ref[...]
    after = normed1 * gain1 + vec[3:4]
    normed2, inverse2 = norm(after + (mlp + vec[4:5]))
    y_out[...] = (normed2 * gain2 + vec[5:6]).astype(BF16)
    dy = cot[...].astype(F32)
    dz2 = norm_back(dy, normed2, inverse2, gain2)
    dz2_ref[...] = dz2
    dm = dz2.astype(BF16)
    mg[at.x, at.c] = dm
    small[1:2] = jnp.sum(dy * normed2, axis=0, keepdims=True)
    small[4:5] = jnp.sum(dm.astype(F32), axis=0, keepdims=True)
    small[5:6] = jnp.sum(dy, axis=0, keepdims=True)
    small[6:8] = jnp.zeros((2, D), F32)

    def mlp_back(x):
        rows = mg[x].reshape(256, D)
        for h in range(2):
            dg = dot_nt(rows[:, 0:256], wr[h, 0, 256:512, :])
            for y in range(1, 4):
                dg += dot_nt(rows[:, 256 * y : 256 * y + 256], wr[h, y, 256:512, :])
            gmid[x, h] = (dg * slope[x, h]).astype(BF16)

    gather_tokens(at, mg, s4, mlp_back)

    def up_back(x, ref):
        for y in range(4):
            part = dot_nt(gmid[x, 0], wr[0, y, 0:256, :]) + dot_nt(gmid[x, 1], wr[1, y, 0:256, :])
            ref[:, :, 256 * y : 256 * y + 256] = part.reshape(2, 128, 256)

    def mlp_weights():
        for h in range(2):
            total = jnp.zeros((1, 256), F32)
            for x in range(4):
                total += jnp.sum(gmid[x, h].astype(F32), axis=0, keepdims=True)
            grad_hidden[h : h + 1] = total
            mid = gmid[:, h].reshape(1024, 256)
            acted = act[:, h].reshape(1024, 256)
            acted_t = acted.T
            for y in range(4):
                cols = slice(256 * y, 256 * y + 256)
                grads[h, y, 256:512, :] = dot(acted_t, mg[:, :, :, cols].reshape(1024, 256)).astype(BF16)
                grads[h, y, 0:256, :] = dot_tn(hg[:, :, :, cols].reshape(1024, 256), mid).astype(BF16)
        grad_hidden[2:8] = jnp.zeros((6, 256), F32)

    dh = dz2_ref[...] + reduce_tokens(
        at, up_back, parts, sc3, rc3, sx3, rx3, fx3, s5, mlp_weights
    )
    normed1 = normed_ref[...]
    dz1 = norm_back(dh, normed1, inverse1, gain1)
    dz1_out[...] = dz1
    da = dz1.astype(BF16)
    ag[at.x, at.c] = da
    small[0:1] = jnp.sum(dh * normed1, axis=0, keepdims=True)
    small[2:3] = jnp.sum(da.astype(F32), axis=0, keepdims=True)
    small[3:4] = jnp.sum(dh, axis=0, keepdims=True)
    sends = []

    def out_back(x):
        rows = ag[x].reshape(256, D)
        both = dot_nt(rows[:, 0:256], wr[:, 0, 512:576, :].reshape(128, 256))
        for y in range(1, 4):
            both += dot_nt(rows[:, 256 * y : 256 * y + 256], wr[:, y, 512:576, :].reshape(128, 256))
        both = both.astype(BF16)
        j = len(sends)
        dctx_out[x * 2 + at.z] = pack(both[:, :64])
        dstage[j] = pack(both[:, 64:])
        send = remote(dstage.at[j], dctx_out.at[x * 2 + at.z], ds, j, at.half)
        send.start()
        sends.append(send)

    gather_tokens(at, ag, s6, out_back)
    c2t = c2[...].reshape(1024, 128).T
    for y in range(4):
        cols = slice(256 * y, 256 * y + 256)
        both = dot(c2t, ag[:, :, :, cols].reshape(1024, 256)).astype(BF16)
        grads[0, y, 512:576, :] = both[:64]
        grads[1, y, 512:576, :] = both[64:]
    for send in swaps:
        send.wait_send()
    for send in sends:
        send.wait()


def last_kernel(
    packed, xg, wq, dz1, dx_out, grads,
    packed_in, both, parts, sc, rc, sx, rx, fx, zs, s1,
):
    at = Place()
    greet([at.core, at.half, at.right, at.left])
    swaps = []
    for j, x in enumerate((at.xo, at.xr, at.xl, at.x)):
        send = remote(packed.at[x * 2 + 1 - at.z], packed_in.at[x], zs, j, at.half)
        send.start()
        swaps.append(send)
    waiting = list(swaps)

    def partial(x, ref):
        waiting.pop(0).wait_recv()
        zero = jnp.zeros((256, 64), BF16)
        for h in range(2):
            pieces = [
                unpack(packed[x * 2 + at.z, t] if h == 0 else packed_in[x, t]) for t in range(3)
            ]
            both[h, x] = jnp.concatenate(pieces + [zero], axis=1)
        for y in range(4):
            part = dot_nt(both[0, x], wq[0, y, 0:256, :]) + dot_nt(both[1, x], wq[1, y, 0:256, :])
            ref[:, :, 256 * y : 256 * y + 256] = part.reshape(2, 128, 256)

    def weights():
        for h in range(2):
            right = both[h].reshape(1024, 256)
            for y in range(4):
                cols = slice(256 * y, 256 * y + 256)
                grads[h, y] = dot_tn(xg[:, :, :, cols].reshape(1024, 256), right).astype(BF16)

    dx_out[...] = dz1[...] + reduce_tokens(at, partial, parts, sc, rc, sx, rx, fx, s1, weights)
    for send in swaps:
        send.wait_send()


def grads_kernel(gq, gr, out, acc, sx, rx, fx, tx, tin, wx, win, ys, zs):
    at = Place()
    greet([at.up, at.down, at.cross, at.twin])
    half = GRAD_ROWS // 2
    first, second = pl.ds(0, half), pl.ds(half, half)

    def own(y):
        return jnp.concatenate([gq[:, y], gr[:, y, 0:576, :]], axis=1)

    sx[0] = own(at.yo)
    oa = remote(sx.at[0, :, first], rx.at[0], ys, 0, at.up)
    ob = remote(sx.at[0, :, second], rx.at[1], ys, 1, at.down)
    oa.start()
    ob.start()
    sx[1] = own(at.yr)
    sx[2] = own(at.yl)
    rb = remote(sx.at[1, :, second], fx.at[0, :, second], ys, 2, at.up)
    la = remote(sx.at[2, :, first], fx.at[1, :, first], ys, 3, at.down)
    rb.start()
    la.start()
    acc[...] = own(at.y).astype(F32)
    oa.wait_recv()
    sx[1, :, first] = (sx[1, :, first].astype(F32) + rx[0].astype(F32)).astype(BF16)
    ra = remote(sx.at[1, :, first], fx.at[0, :, first], ys, 4, at.up)
    ra.start()
    ob.wait_recv()
    sx[2, :, second] = (sx[2, :, second].astype(F32) + rx[1].astype(F32)).astype(BF16)
    lb = remote(sx.at[2, :, second], fx.at[1, :, second], ys, 5, at.down)
    lb.start()
    for each in (rb, la, ra, lb):
        each.wait_recv()
    acc[...] += fx[0].astype(F32) + fx[1].astype(F32)
    tx[...] = acc[1].astype(BF16)
    t = remote(tx, tin, zs, 0, at.cross)
    t.start()
    t.wait_recv()
    total = acc[0] + tin[...].astype(F32)
    wx[...] = total.astype(BF16)
    w = remote(wx, win, zs, 1, at.twin)
    w.start()
    w.wait_recv()
    out[...] = wx[...].astype(F32) + win[...].astype(F32)
    for each in (oa, ob, rb, la, ra, lb, t, w):
        each.wait_send()


def call(kernel, name, collective, n_in, outs, scratch):
    specs = [pl.BlockSpec(memory_space=VMEM)] * n_in
    return pl.pallas_call(
        kernel,
        out_shape=[jax.ShapeDtypeStruct(shape, kind) for shape, kind in outs],
        in_specs=specs,
        out_specs=[pl.BlockSpec(memory_space=VMEM)] * len(outs),
        scratch_shapes=scratch,
        compiler_params=pltpu.CompilerParams(
            collective_id=collective, has_side_effects=True, vmem_limit_bytes=56 << 20
        ),
        name=name,
    )


def per_device(
    inputs, w_qkv, b_qv, w_out, w_in, b_in, down_weight, norm_gains, shifts, bias_table, buckets, cotangent
):
    x = inputs[0]
    zero64 = jnp.zeros((64,), BF16)
    bias_rows = jnp.zeros((16, 256), BF16)
    wq_own = jnp.concatenate(
        [
            jnp.pad(w_qkv[0].reshape(256, 192), ((0, 0), (0, 64))),
            bias_rows.at[0].set(jnp.concatenate([b_qv[0, 0], zero64, b_qv[0, 1], zero64])),
        ],
        axis=0,
    )
    wr_own = jnp.concatenate(
        [w_in[0], down_weight[0], w_out[0], bias_rows.at[0].set(b_in[0])], axis=0
    )
    xg, wq, wr, packed = call(
        project_kernel,
        "project",
        0,
        3,
        [
            ((4, 2, 128, D), BF16),
            ((2, 4, WQ_ROWS, 256), BF16),
            ((2, 4, WR_ROWS, 256), BF16),
            ((8, 3, 128, 128), BF16),
        ],
        [
            VMEM((4, 3, 128, 128), BF16),
            SEMS((2, 10)),
            SEMS((2, 13)),
            SEMS((2, 13)),
            SEMS((2, 4)),
        ],
    )(x, wq_own, wr_own)

    onehot = (buckets[0][None, :] == jnp.arange(BUCKETS, dtype=jnp.int32)[:, None]).astype(F32)
    onehot = jnp.pad(onehot, ((0, 0), (0, 1)))
    relative = jnp.sum(onehot * bias_table[0].astype(F32), axis=0)
    seed = jnp.stack([jnp.roll(relative, r - 255) for r in range(8)])

    whole = lambda shape: pl.BlockSpec(shape, lambda i: (0,) * len(shape))
    probs, context, context_packed = pl.pallas_call(
        attend_kernel,
        grid=(8,),
        out_shape=[
            jax.ShapeDtypeStruct((LENGTH, LENGTH), BF16),
            jax.ShapeDtypeStruct((LENGTH, 64), F32),
            jax.ShapeDtypeStruct((8, 128, 128), BF16),
        ],
        in_specs=[whole((8, 3, 128, 128)), whole((8, BAND))],
        out_specs=[
            pl.BlockSpec((STRIP, LENGTH), lambda i: (i, 0)),
            pl.BlockSpec((STRIP, 64), lambda i: (i, 0)),
            pl.BlockSpec((1, 128, 128), lambda i: (i, 0, 0)),
        ],
        scratch_shapes=[VMEM((STRIP, BAND), F32), VMEM((LENGTH, 64), BF16), VMEM((LENGTH, 64), BF16)],
        compiler_params=pltpu.CompilerParams(vmem_limit_bytes=50 << 20),
        name="attend",
    )(packed, seed)

    vectors = jnp.concatenate([norm_gains[0], shifts[0], jnp.zeros((2, D), BF16)], axis=0).astype(F32)
    reduce_bufs = [*REDUCE_SCRATCH] * 3
    y, dz1, dctx, grads_r, small, grad_hidden = call(
        middle_kernel,
        "middle",
        1,
        5,
        [
            ((128, D), BF16),
            ((128, D), F32),
            ((8, 128, 128), BF16),
            ((2, 4, WR_ROWS, 256), BF16),
            ((8, D), F32),
            ((8, 256), F32),
        ],
        [
            VMEM((4, 128, 128), BF16),
            VMEM((4, 2, 128, 128), BF16),
            VMEM((4, 2, 128, D), BF16),
            VMEM((4, 2, 128, D), BF16),
            VMEM((4, 2, 128, D), BF16),
            VMEM((4, 2, 256, 256), BF16),
            VMEM((4, 2, 256, 256), F32),
            VMEM((4, 2, 256, 256), BF16),
            VMEM((4, 2, 128, D), F32),
            *reduce_bufs,
            VMEM((128, D), F32),
            VMEM((128, D), F32),
            VMEM((4, 128, 128), BF16),
            SEMS((2, 4)),
            *[SEMS((2, 10))] * 6,
            SEMS((2, 4)),
        ],
    )(context_packed, x, cotangent[0], wr, vectors)

    out_packed, fold, sums = pl.pallas_call(
        attend_back_kernel,
        grid=(8,),
        out_shape=[
            jax.ShapeDtypeStruct((8, 3, 128, 128), BF16),
            jax.ShapeDtypeStruct((8, BAND), F32),
            jax.ShapeDtypeStruct((8, 128), F32),
        ],
        in_specs=[
            whole((8, 3, 128, 128)),
            pl.BlockSpec((STRIP, LENGTH), lambda i: (i, 0)),
            pl.BlockSpec((STRIP, 64), lambda i: (i, 0)),
            whole((8, 128, 128)),
        ],
        out_specs=[whole((8, 3, 128, 128)), whole((8, BAND)), whole((8, 128))],
        scratch_shapes=[
            VMEM((STRIP, BAND), F32),
            VMEM((LENGTH, 64), BF16),
            VMEM((LENGTH, 64), BF16),
            VMEM((64, LENGTH), F32),
            VMEM((64, LENGTH), F32),
            VMEM((8, STRIP, 64), BF16),
        ],
        compiler_params=pltpu.CompilerParams(vmem_limit_bytes=50 << 20),
        name="attend_back",
    )(packed, probs, context, dctx)

    dx, grads_q = call(
        last_kernel,
        "last",
        2,
        4,
        [((128, D), F32), ((2, 4, 256, 256), BF16)],
        [
            VMEM((4, 3, 128, 128), BF16),
            VMEM((2, 4, 256, 256), BF16),
            VMEM((4, 2, 128, D), F32),
            *REDUCE_SCRATCH,
            SEMS((2, 4)),
            SEMS((2, 10)),
        ],
    )(out_packed, xg, wq, dz1)

    (summed,) = call(
        grads_kernel,
        "grads",
        3,
        2,
        [((GRAD_ROWS, 256), F32)],
        [
            VMEM((2, GRAD_ROWS, 256), F32),
            VMEM((3, 2, GRAD_ROWS, 256), BF16),
            VMEM((2, 2, GRAD_ROWS // 2, 256), BF16),
            VMEM((2, 2, GRAD_ROWS, 256), BF16),
            VMEM((GRAD_ROWS, 256), BF16),
            VMEM((GRAD_ROWS, 256), BF16),
            VMEM((GRAD_ROWS, 256), BF16),
            VMEM((GRAD_ROWS, 256), BF16),
            SEMS((2, 6)),
            SEMS((2, 2)),
        ],
    )(grads_q, grads_r)

    grad_band = sum(jnp.roll(fold[r], 255 - r) for r in range(8))
    table = jnp.sum(onehot * grad_band, axis=1)
    hidden_other = lax.ppermute(grad_hidden[1], "mp", [(m, m ^ 2) for m in range(16)])
    small_sum = lax.psum(small, ("replica", "fsdp", "mp"))
    pair, unit, table = lax.psum(
        (sums[0].reshape(1, 2, 64), (grad_hidden[0] + hidden_other)[None], table[None, :, None]),
        ("replica", "fsdp"),
    )
    return (
        y[None],
        dx[None],
        summed[0:256, 0:192].reshape(1, 256, 3, 64),
        pair,
        summed[768:832][None],
        summed[256:512][None],
        unit,
        summed[512:768][None],
        small_sum[None, 0:2],
        small_sum[None, 2:6],
        table,
    )


def solution(mesh):
    tokens = P(("replica", "fsdp"), "mp", None)
    qkv, outer, up, down = P(None, "fsdp", None, "mp"), P(None, "mp", "fsdp"), P(None, "fsdp", "mp"), P(None, "mp", "fsdp")
    return jax.shard_map(
        per_device,
        mesh=mesh,
        in_specs=(
            tokens, qkv, P(None, None, "mp"), outer, up, P(None, "mp"), down, P(), P(),
            P(None, None, "mp"), P(("replica", "fsdp"), None), tokens,
        ),
        out_specs=(
            tokens, tokens, qkv, P(None, None, "mp"), outer, up, P(None, "mp"), down, P(), P(), P(None, None, "mp"),
        ),
        check_vma=False,
    )
```

```python
import jax
import jax.numpy as jnp
from jax import lax
from jax.experimental import pallas as pl
from jax.experimental.pallas import tpu as pltpu
from jax.sharding import PartitionSpec as P

D = 1024
HEAD_DIM = 64
BUCKETS = 32
EPSILON = 1e-05
LENGTH = 2048
STRIP = 256
BAND = 4096
WQ_ROWS = 272
WR_ROWS = 592
VMEM = pltpu.VMEM
BF16 = jnp.bfloat16
F32 = jnp.float32
MESH = pl.DeviceIdType.MESH
SEMS = pltpu.SemaphoreType.DMA


class Place:
    def __init__(self):
        rep, row, mp = (lax.axis_index(a) for a in ("replica", "fsdp", "mp"))
        self.rep, self.y = rep, row
        self.x, self.z, self.c = mp // 4, (mp // 2) % 2, mp % 2
        self.xr, self.xl, self.xo = (self.x + 1) % 4, (self.x + 3) % 4, (self.x + 2) % 4
        self.yr, self.yl, self.yo = (row + 1) % 4, (row + 3) % 4, (row + 2) % 4

        def at(rep=rep, y=row, x=self.x, z=self.z, c=self.c):
            return (rep, y, x * 4 + z * 2 + c)

        self.core = at(c=1 - self.c)
        self.half = at(z=1 - self.z)
        self.right, self.left = at(x=self.xr), at(x=self.xl)
        self.up, self.down = at(y=self.yr), at(y=self.yl)
        self.far_x, self.far_y = at(x=self.xo), at(y=self.yo)
        self.twin = at(rep=1 - rep)
        self.cross = at(rep=1 - rep, z=1 - self.z)


def greet(partners):
    barrier = pltpu.get_barrier_semaphore()
    for partner in partners:
        pl.semaphore_signal(barrier, inc=1, device_id=partner, device_id_type=MESH)
    pl.semaphore_wait(barrier, len(partners))


def remote(src, dst, sems, index, partner):
    return pltpu.make_async_remote_copy(
        src_ref=src,
        dst_ref=dst,
        send_sem=sems.at[0, index],
        recv_sem=sems.at[1, index],
        device_id=partner,
        device_id_type=MESH,
    )


def dot(a, b):
    return lax.dot_general(a, b, (((1,), (0,)), ((), ())), preferred_element_type=F32)


def dot_nt(a, b):
    return lax.dot_general(a, b, (((1,), (1,)), ((), ())), preferred_element_type=F32)


def dot_tn(a, b):
    return lax.dot_general(a, b, (((0,), (0,)), ((), ())), preferred_element_type=F32)


def gather_tokens(at, buf, sems, process, before=None):
    first, second, whole = pl.ds(0, 64), pl.ds(64, 64), pl.ds(0, 128)

    def copy(index, x, rows, partner):
        ref = buf.at[x, at.c, rows]
        return remote(ref, ref, sems, index, partner)

    c0 = copy(0, at.x, whole, at.core)
    a1, a2 = copy(1, at.x, first, at.right), copy(2, at.x, second, at.right)
    b1, b2 = copy(3, at.x, second, at.left), copy(4, at.x, first, at.left)
    f5, f6 = copy(5, at.xl, first, at.right), copy(6, at.xr, second, at.left)
    c7, c8 = copy(7, at.xl, whole, at.core), copy(8, at.xr, whole, at.core)
    c9 = copy(9, at.xo, whole, at.core)
    for each in (a1, b1, a2, b2, c0):
        each.start()
    if before is None:
        c0.wait_recv()
        process(at.x)
    a1.wait_recv()
    f5.start()
    b1.wait_recv()
    f6.start()
    if before is not None:
        before()
        c0.wait_recv()
        process(at.x)
    a2.wait_recv()
    c7.start()
    b2.wait_recv()
    c8.start()
    c7.wait_recv()
    process(at.xl)
    c8.wait_recv()
    process(at.xr)
    f5.wait_recv()
    f6.wait_recv()
    c9.start()
    c9.wait_recv()
    process(at.xo)
    for each in (c0, a1, a2, b1, b2, f5, f6, c7, c8, c9):
        each.wait_send()


def reduce_tokens(at, produce, parts, sc, rc, sx, rx, fx, sems, hooks=()):
    first, second = pl.ds(0, 64), pl.ds(64, 64)
    cores = []

    def make(j, x):
        produce(x, parts.at[j])
        sc[j] = parts[j, 1 - at.c].astype(BF16)
        cores.append(remote(sc.at[j], rc.at[j], sems, j, at.core))
        cores[j].start()

    make(0, at.xo)
    make(1, at.xr)
    cores[0].wait_recv()
    sx[0] = (parts[0, at.c] + rc[0].astype(F32)).astype(BF16)
    oa = remote(sx.at[0, first], rx.at[0], sems, 4, at.right)
    ob = remote(sx.at[0, second], rx.at[1], sems, 5, at.left)
    oa.start()
    ob.start()
    make(2, at.xl)
    cores[1].wait_recv()
    sx[1, second] = (parts[1, at.c, second] + rc[1, second].astype(F32)).astype(BF16)
    rb = remote(sx.at[1, second], fx.at[0, second], sems, 6, at.right)
    rb.start()
    cores[2].wait_recv()
    sx[2, first] = (parts[2, at.c, first] + rc[2, first].astype(F32)).astype(BF16)
    la = remote(sx.at[2, first], fx.at[1, first], sems, 7, at.left)
    la.start()
    make(3, at.x)
    oa.wait_recv()
    sx[1, first] = (parts[1, at.c, first] + rc[1, first].astype(F32) + rx[0].astype(F32)).astype(BF16)
    ra = remote(sx.at[1, first], fx.at[0, first], sems, 8, at.right)
    ra.start()
    ob.wait_recv()
    sx[2, second] = (
        parts[2, at.c, second] + rc[2, second].astype(F32) + rx[1].astype(F32)
    ).astype(BF16)
    lb = remote(sx.at[2, second], fx.at[1, second], sems, 9, at.left)
    lb.start()
    for hook in hooks:
        hook()
    cores[3].wait_recv()
    for each in (rb, la, ra, lb):
        each.wait_recv()
    total = parts[3, at.c] + rc[3].astype(F32) + fx[0].astype(F32) + fx[1].astype(F32)
    for each in cores + [oa, ob, rb, la, ra, lb]:
        each.wait_send()
    return total


REDUCE_SCRATCH = [
    VMEM((4, 128, D), BF16),
    VMEM((4, 128, D), BF16),
    VMEM((3, 128, D), BF16),
    VMEM((2, 64, D), BF16),
    VMEM((2, 128, D), BF16),
]


class GatherRows:
    def __init__(self, at, buf, sems, rows):
        split = rows // 32 * 16
        first, second = pl.ds(0, split), pl.ds(split, rows - split)

        def copy(index, half, y, rows_, partner):
            ref = buf.at[half, y, rows_]
            return remote(ref, ref, sems, index, partner)

        whole = pl.ds(0, rows)
        self.cross = remote(buf.at[0, at.y, whole], buf.at[1, at.y, whole], sems, 0, at.cross)
        self.sets = []
        for h in range(2):
            b = 1 + 6 * h
            self.sets.append(
                (
                    copy(b, h, at.y, first, at.up),
                    copy(b + 1, h, at.y, second, at.down),
                    copy(b + 2, h, at.y, second, at.up),
                    copy(b + 3, h, at.y, first, at.down),
                    copy(b + 4, h, at.yl, first, at.up),
                    copy(b + 5, h, at.yr, second, at.down),
                )
            )

    def step0(self):
        self.cross.start()
        for each in self.sets[0][:4]:
            each.start()

    def step1(self):
        self.cross.wait_recv()
        for each in self.sets[1][:4]:
            each.start()

    def forward(self, h):
        s = self.sets[h]
        s[0].wait_recv()
        s[4].start()
        s[1].wait_recv()
        s[5].start()

    def finish(self):
        for s in self.sets:
            for each in s[2:]:
                each.wait_recv()
        self.cross.wait_send()
        for s in self.sets:
            for each in s:
                each.wait_send()


def unpack(pair):
    return jnp.concatenate([pair[:, :64], pair[:, 64:]], axis=0)


def pack(rows):
    return jnp.concatenate([rows[:128], rows[128:]], axis=1)


class SumAll:
    def __init__(self, buf, sems, slot, partners):
        self.buf = buf
        ref = buf.at[slot]
        self.copies = [remote(ref, ref, sems, i, partner) for i, partner in enumerate(partners)]

    def start(self):
        for each in self.copies:
            each.start()

    def finish(self):
        for each in self.copies:
            each.wait()
        total = self.buf[0]
        for i in range(1, len(self.copies) + 1):
            total = total + self.buf[i]
        return total


class ReduceRows:
    def __init__(self, at, src, sx, rx, fx, acc, tx, tin, wx, win, ys, zs):
        rows = src.shape[2]
        first, second = pl.ds(0, rows // 2), pl.ds(rows // 2, rows // 2)
        self.at, self.src, self.sx, self.rx, self.fx, self.acc = at, src, sx, rx, fx, acc
        self.first, self.second = first, second
        self.tx, self.tin, self.wx, self.win = tx, tin, wx, win
        self.oa = remote(src.at[:, at.yo, first], rx.at[0], ys, 0, at.up)
        self.ob = remote(src.at[:, at.yo, second], rx.at[1], ys, 1, at.down)
        self.rb = remote(src.at[:, at.yr, second], fx.at[0, :, second], ys, 2, at.up)
        self.la = remote(src.at[:, at.yl, first], fx.at[1, :, first], ys, 3, at.down)
        self.ra = remote(sx.at[0], fx.at[0, :, first], ys, 4, at.up)
        self.lb = remote(sx.at[1], fx.at[1, :, second], ys, 5, at.down)
        self.t = remote(tx, tin, zs, 0, at.cross)
        self.w = remote(wx, win, zs, 1, at.twin)

    def step0(self):
        for each in (self.oa, self.ob, self.rb, self.la):
            each.start()

    def step1(self):
        self.oa.wait_recv()
        self.sx[0] = (
            self.src[:, self.at.yr, self.first].astype(F32) + self.rx[0].astype(F32)
        ).astype(BF16)
        self.ra.start()
        self.ob.wait_recv()
        self.sx[1] = (
            self.src[:, self.at.yl, self.second].astype(F32) + self.rx[1].astype(F32)
        ).astype(BF16)
        self.lb.start()

    def step2(self):
        for each in (self.rb, self.la, self.ra, self.lb):
            each.wait_recv()
        fx = self.fx
        self.tx[...] = (
            self.src[1, self.at.y].astype(F32) + fx[0, 1].astype(F32) + fx[1, 1].astype(F32)
        ).astype(BF16)
        self.t.start()
        self.acc[...] = (
            self.src[0, self.at.y].astype(F32) + fx[0, 0].astype(F32) + fx[1, 0].astype(F32)
        )

    def step3(self):
        self.t.wait_recv()
        self.wx[...] = (self.acc[...] + self.tin[...].astype(F32)).astype(BF16)
        self.w.start()

    def step4(self):
        self.w.wait_recv()
        for each in (self.oa, self.ob, self.rb, self.la, self.ra, self.lb, self.t, self.w):
            each.wait_send()

    def rows(self, rows):
        return self.wx[rows].astype(F32) + self.win[rows].astype(F32)


def reduce_rows_scratch(rows):
    return [
        VMEM((2, 2, rows // 2, 256), BF16),
        VMEM((2, 2, rows // 2, 256), BF16),
        VMEM((2, 2, rows, 256), BF16),
        VMEM((rows, 256), F32),
        *[VMEM((rows, 256), BF16)] * 4,
        SEMS((2, 6)),
        SEMS((2, 2)),
    ]


def load_heads(packed, keys, values):
    for i in range(8):
        keys[256 * i : 256 * i + 256] = unpack(packed[i, 1])
        values[256 * i : 256 * i + 256] = unpack(packed[i, 2])


def front_kernel(
    x_ref, w_qkv, b_qv, w_out, w_in, w_back, b_in, table, buckets,
    xg, wq, wr, packed, probs_out, context, context_packed,
    stage, band, keys, values, probs, xs, qs, rs, zs, ps,
):
    at = Place()
    greet([at.core, at.half, at.cross, at.right, at.left, at.up, at.down])
    xg[at.x, at.c] = x_ref[...]
    wq[0, at.y, 0:256, 0:192] = w_qkv[...]
    wq[0, at.y, 0:256, 192:256] = jnp.zeros((256, 64), BF16)
    none = jnp.zeros((1, 64), BF16)
    pair = jnp.concatenate([b_qv[0:1], none, b_qv[1:2], none], axis=1)
    wq[0, at.y, 256:272, :] = jnp.broadcast_to(pair, (16, 256))
    gq = GatherRows(at, wq, qs, WQ_ROWS)
    gr = GatherRows(at, wr, rs, WR_ROWS)
    sends = []

    def weights():
        wr[0, at.y, 0:256] = w_in[...]
        wr[0, at.y, 256:512] = w_back[...]
        wr[0, at.y, 512:576] = w_out[...]
        wr[0, at.y, 576:592] = jnp.broadcast_to(b_in[...], (16, 256))
        gq.step1()
        gq.forward(0)
        relative = jnp.zeros((8, BAND), F32)
        bucket = jnp.broadcast_to(buckets[...], (8, BAND))
        for b in range(BUCKETS):
            value = table[b : b + 1, 0:1].astype(F32)
            relative = jnp.where(bucket == b, value, relative)
        for r in range(8):
            band[r : r + 1] = pltpu.roll(relative[0:1], (r - 255) % BAND, 1)
        gq.forward(1)
        gr.step0()
        size = 8
        while size < STRIP:
            band[size : 2 * size] = pltpu.roll(band[0:size], size, 1)
            size *= 2
        gq.finish()

    def process(x):
        rows = xg[x].reshape(256, D)
        j = len(sends)
        for h in range(2):
            weight = wq[h, :, 0:256, :].reshape(D, 256)
            bias = wq[h, at.y, 256:272, :].astype(F32)[0:1]
            out = (dot(rows, weight) + bias).astype(BF16)
            for t in range(3):
                part = pack(out[:, 64 * t : 64 * t + 64])
                if h == 0:
                    packed[x * 2 + at.z, t] = part
                else:
                    stage[j, t] = part
        send = remote(stage.at[j], packed.at[x * 2 + at.z], zs, j, at.half)
        send.start()
        sends.append(send)

    gq.step0()
    gather_tokens(at, xg, xs, process, weights)
    gr.step1()
    for send in sends:
        send.wait()
    load_heads(packed, keys, values)

    def strip(step):
        query = unpack(packed[step, 0]) * jnp.asarray(0.125, BF16)
        offset = pl.multiple_of((7 - step) * STRIP, STRIP)
        scores = dot_nt(query, keys[...]) + band[:, pl.ds(offset, LENGTH)]
        peak = jnp.max(scores, axis=1, keepdims=True)
        powers = jnp.exp(scores - peak)
        total = jnp.sum(powers, axis=1, keepdims=True)
        prob = (powers * (1.0 / total)).astype(BF16)
        probs[step] = prob
        pltpu.make_async_copy(probs.at[step], probs_out.at[step], ps.at[step]).start()
        out = dot(prob, values[...])
        context[pl.ds(pl.multiple_of(step * STRIP, STRIP), STRIP)] = out
        context_packed[step] = pack(out.astype(BF16))

    for first, hook in ((0, lambda: gr.forward(0)), (4, lambda: gr.forward(1))):
        pl.loop(first, first + 4)(strip)
        hook()
    gr.finish()
    for step in range(8):
        pltpu.make_async_copy(probs.at[step], probs_out.at[step], ps.at[step]).wait()


def back_kernel(
    packed, context, dctx, probs_in, xg, wq, dz1, grads_r, small, buckets,
    dx_out, g_in, g_back, g_out, g_qkv, small_out, pair_out, unit_out, table_out,
    probs, out_packed, packed_in, both, grads_q, parts,
    band, keys, values, grad_keys, grad_values, grad_query,
    core_buf, x_buf, y_buf, z_buf, pair_buf, twin_buf,
    sc, rc, sx, rx, fx,
    rsx, rrx, rfx, racc, rtx, rtin, rwx, rwin, rys, rzs,
    qsx, qrx, qfx, qacc, qtx, qtin, qwx, qwin, qys, qzs,
    ps, zs, s1, core_s, x_s, y_s, z_s, pair_s, twin_s,
):
    at = Place()
    for step in range(8):
        pltpu.make_async_copy(probs_in.at[step], probs.at[step], ps.at[step]).start()
    greet(
        [at.core, at.half, at.cross, at.twin, at.right, at.left, at.up, at.down, at.far_x, at.far_y]
    )
    reduce_r = ReduceRows(at, grads_r, rsx, rrx, rfx, racc, rtx, rtin, rwx, rwin, rys, rzs)
    reduce_q = ReduceRows(at, grads_q, qsx, qrx, qfx, qacc, qtx, qtin, qwx, qwin, qys, qzs)
    reduce_r.step0()
    z_slot = at.z * 2 + at.rep
    core_sum = SumAll(core_buf, core_s, at.c, [at.core])
    x_sum = SumAll(x_buf, x_s, at.x, [at.right, at.left, at.far_x])
    y_sum = SumAll(y_buf, y_s, at.y, [at.up, at.down, at.far_y])
    z_sum = SumAll(z_buf, z_s, z_slot, [at.half, at.twin, at.cross])
    pair_sum = SumAll(pair_buf, pair_s, at.y, [at.up, at.down, at.far_y])
    twin_sum = SumAll(twin_buf, twin_s, at.rep, [at.twin])
    core_buf[at.c] = small[:, 0:D]
    core_sum.start()
    band[...] = jnp.zeros_like(band)
    grad_keys[...] = jnp.zeros_like(grad_keys)
    grad_values[...] = jnp.zeros_like(grad_values)
    load_heads(packed, keys, values)

    def strip(step):
        pltpu.make_async_copy(probs_in.at[step], probs.at[step], ps.at[step]).wait()
        query = unpack(packed[step, 0]) * jnp.asarray(0.125, BF16)
        upstream = unpack(dctx[step])
        prob = probs[step]
        rows = pl.ds(pl.multiple_of(step * STRIP, STRIP), STRIP)
        dots = jnp.sum(upstream.astype(F32) * context[rows], axis=1, keepdims=True)
        grad_scores = prob.astype(F32) * (dot_nt(upstream, values[...]) - dots)
        offset = pl.multiple_of((7 - step) * STRIP, STRIP)
        band[:, pl.ds(offset, LENGTH)] += grad_scores
        low = grad_scores.astype(BF16)
        gq = (dot(low, keys[...]) * 0.125).astype(BF16)
        grad_query[step] = gq
        out_packed[step, 0] = pack(gq)
        grad_keys[...] += dot(query.T, low)
        grad_values[...] += dot(upstream.T, prob)

    query_sends = []

    def hook(index):
        src = out_packed.at[2 * index + 1 - at.z, 0]
        send = remote(src, packed_in.at[index, 0], zs, index, at.half)
        send.start()
        query_sends.append(send)
        if index == 0:
            x_buf[at.x] = core_sum.finish()
            x_sum.start()
        elif index == 1:
            y_buf[at.y, :, 0:D] = x_sum.finish()
            y_buf[at.y, :, D : D + 256] = small[:, D : D + 256]
            y_sum.start()
        elif index == 2:
            z_buf[z_slot] = y_sum.finish()
            z_sum.start()
            reduce_r.step1()
        else:
            total = z_sum.finish()
            small_out[...] = total[:, 0:D]
            hidden = jnp.where(at.z == 0, total[0:1, D : D + 256], total[1:2, D : D + 256])
            unit_out[...] = jnp.broadcast_to(hidden, (8, 256))

    for index in range(4):
        pl.loop(2 * index, 2 * index + 2)(strip)
        hook(index)

    total_v = jnp.zeros((1, 64), F32)
    total_q = jnp.zeros((1, 64), F32)
    for i in range(8):
        cols = slice(256 * i, 256 * i + 256)
        out_packed[i, 1] = pack(grad_keys[:, cols].T.astype(BF16))
        gv = grad_values[:, cols].T.astype(BF16)
        total_q += jnp.sum(grad_query[i].astype(F32), axis=0, keepdims=True)
        total_v += jnp.sum(gv.astype(F32), axis=0, keepdims=True)
        out_packed[i, 2] = pack(gv)
    order = (at.xo, at.xr, at.xl, at.x)
    swaps = []
    for j, x in enumerate(order):
        src = out_packed.at[2 * x + 1 - at.z, 1:3]
        send = remote(src, packed_in.at[x, 1:3], zs, 4 + j, at.half)
        send.start()
        swaps.append(send)

    size = STRIP // 2
    while size >= 8:
        band[0:size] = band[0:size] + pltpu.roll(band[size : 2 * size], BAND - size, 1)
        size //= 2
    line = pltpu.roll(band[0:1], 255, 1)
    for r in range(1, 8):
        line = line + pltpu.roll(band[r : r + 1], 255 - r, 1)
    bucket = buckets[...]
    pair_buf[at.y, 0:8] = jnp.broadcast_to(jnp.concatenate([total_q, total_v], axis=1), (8, 128))
    for b in range(BUCKETS):
        total = jnp.sum(jnp.where(bucket == b, line, 0.0), axis=1, keepdims=True)
        pair_buf[at.y, 8 + b : 9 + b] = jnp.broadcast_to(total, (1, 128))
    pair_sum.start()
    reduce_r.step2()

    for send in query_sends:
        send.wait()
    zero = jnp.zeros((256, 64), BF16)
    for j, x in enumerate(order):
        for h in range(2):
            if h == 1:
                swaps[j].wait()
            ref = out_packed.at[x * 2 + at.z] if h == 0 else packed_in.at[x]
            both[h, x] = jnp.concatenate([unpack(ref[t]) for t in range(3)] + [zero], axis=1)
    for h in range(2):
        right = both[h].reshape(1024, 256)
        for y in range(4):
            cols = slice(256 * y, 256 * y + 256)
            grads_q[h, y] = dot_tn(xg[:, :, :, cols].reshape(1024, 256), right).astype(BF16)
    reduce_q.step0()
    reduce_r.step3()

    def partial(x, ref):
        for y in range(4):
            part = dot_nt(both[0, x], wq[0, y, 0:256, :]) + dot_nt(both[1, x], wq[1, y, 0:256, :])
            ref[:, :, 256 * y : 256 * y + 256] = part.reshape(2, 128, 256)

    def later():
        reduce_q.step1()
        twin_buf[at.rep] = pair_sum.finish()
        twin_sum.start()

    total = reduce_tokens(at, partial, parts, sc, rc, sx, rx, fx, s1, [later])
    dx_out[...] = dz1[...] + total
    reduce_q.step2()
    pair = twin_sum.finish()
    pair_out[...] = pair[0:8]
    table_out[...] = pair[8:40]
    reduce_r.step4()
    g_in[...] = reduce_r.rows(pl.ds(0, 256))
    g_back[...] = reduce_r.rows(pl.ds(256, 256))
    g_out[...] = reduce_r.rows(pl.ds(512, 64))
    reduce_q.step3()
    reduce_q.step4()
    g_qkv[...] = reduce_q.rows(pl.ds(0, 256))[:, 0:192]


def norm(values):
    center = values - jnp.mean(values, axis=-1, keepdims=True)
    inverse = lax.rsqrt(jnp.mean(center * center, axis=-1, keepdims=True) + EPSILON)
    return center * inverse, inverse


def norm_back(upstream, normed, inverse, gain):
    scaled = upstream * gain
    return inverse * (
        scaled
        - jnp.mean(scaled, axis=-1, keepdims=True)
        - normed * jnp.mean(scaled * normed, axis=-1, keepdims=True)
    )


def middle_kernel(
    ctx, x_ref, cot, wr, vectors,
    y_out, dz1_out, dctx_out, grads, small,
    ctx_in, c2, hg, mg, ag, act, slope, gmid, parts,
    sc1, rc1, sx1, rx1, fx1, sc2, rc2, sx2, rx2, fx2, sc3, rc3, sx3, rx3, fx3,
    normed_ref, dz2_ref, dstage,
    zs, s1, s2, s3, s4, s5, s6, ds,
):
    at = Place()
    greet([at.core, at.half, at.right, at.left])
    swaps = []
    for j, x in enumerate((at.xo, at.xr, at.xl, at.x)):
        send = remote(ctx.at[x * 2 + 1 - at.z], ctx_in.at[x], zs, j, at.half)
        send.start()
        swaps.append(send)
    waiting = list(swaps)

    def out_partial(x, ref):
        waiting.pop(0).wait_recv()
        own, other = ctx[x * 2 + at.z], ctx_in[x]
        c2[x, 0] = jnp.concatenate([own[:, :64], other[:, :64]], axis=1)
        c2[x, 1] = jnp.concatenate([own[:, 64:], other[:, 64:]], axis=1)
        rows = c2[x].reshape(256, 128)
        for y in range(4):
            weight = wr[:, y, 512:576, :].reshape(128, 256)
            ref[:, :, 256 * y : 256 * y + 256] = dot(rows, weight).reshape(2, 128, 256)

    attended = reduce_tokens(at, out_partial, parts, sc1, rc1, sx1, rx1, fx1, s1)
    vec = vectors[...]
    gain1, gain2 = vec[0:1], vec[1:2]
    normed1, inverse1 = norm(x_ref[...].astype(F32) + (attended + vec[2:3]))
    normed_ref[...] = normed1
    after = normed1 * gain1 + vec[3:4]
    hg[at.x, at.c] = after.astype(BF16)

    def mlp_up(x):
        rows = hg[x].reshape(256, D)
        for h in range(2):
            weight = wr[h, :, 0:256, :].reshape(D, 256)
            bias = wr[h, at.y, 576:592, :].astype(F32)[0:1]
            u = dot(rows, weight) + bias
            phi = 0.5 * (1.0 + lax.erf(u * 0.7071067811865476))
            act[x, h] = (u * phi).astype(BF16)
            slope[x, h] = phi + u * (jnp.exp(-0.5 * u * u) * 0.3989422804014327)

    gather_tokens(at, hg, s2, mlp_up)

    def mlp_down(x, ref):
        for y in range(4):
            part = dot(act[x, 0], wr[0, y, 256:512, :]) + dot(act[x, 1], wr[1, y, 256:512, :])
            ref[:, :, 256 * y : 256 * y + 256] = part.reshape(2, 128, 256)

    mlp = reduce_tokens(at, mlp_down, parts, sc2, rc2, sx2, rx2, fx2, s3)
    normed1 = normed_ref[...]
    after = normed1 * gain1 + vec[3:4]
    normed2, inverse2 = norm(after + (mlp + vec[4:5]))
    y_out[...] = (normed2 * gain2 + vec[5:6]).astype(BF16)
    dy = cot[...].astype(F32)
    dz2 = norm_back(dy, normed2, inverse2, gain2)
    dz2_ref[...] = dz2
    dm = dz2.astype(BF16)
    mg[at.x, at.c] = dm
    small[1:2, 0:D] = jnp.sum(dy * normed2, axis=0, keepdims=True)
    small[4:5, 0:D] = jnp.sum(dm.astype(F32), axis=0, keepdims=True)
    small[5:6, 0:D] = jnp.sum(dy, axis=0, keepdims=True)
    small[6:8, 0:D] = jnp.zeros((2, D), F32)

    def mlp_back(x):
        rows = mg[x].reshape(256, D)
        for h in range(2):
            dg = dot_nt(rows[:, 0:256], wr[h, 0, 256:512, :])
            for y in range(1, 4):
                dg += dot_nt(rows[:, 256 * y : 256 * y + 256], wr[h, y, 256:512, :])
            gmid[x, h] = (dg * slope[x, h]).astype(BF16)

    gather_tokens(at, mg, s4, mlp_back)

    def up_back(x, ref):
        for y in range(4):
            part = dot_nt(gmid[x, 0], wr[0, y, 0:256, :]) + dot_nt(gmid[x, 1], wr[1, y, 0:256, :])
            ref[:, :, 256 * y : 256 * y + 256] = part.reshape(2, 128, 256)

    def mlp_weights():
        hidden = []
        for h in range(2):
            total = jnp.zeros((1, 256), F32)
            for x in range(4):
                total += jnp.sum(gmid[x, h].astype(F32), axis=0, keepdims=True)
            hidden.append(total)
            mid = gmid[:, h].reshape(1024, 256)
            acted = act[:, h].reshape(1024, 256)
            acted_t = acted.T
            for y in range(4):
                cols = slice(256 * y, 256 * y + 256)
                grads[h, y, 256:512, :] = dot(acted_t, mg[:, :, :, cols].reshape(1024, 256)).astype(BF16)
                grads[h, y, 0:256, :] = dot_tn(hg[:, :, :, cols].reshape(1024, 256), mid).astype(BF16)
        small[0:1, D : D + 256] = jnp.where(at.z == 0, hidden[0], hidden[1])
        small[1:2, D : D + 256] = jnp.where(at.z == 0, hidden[1], hidden[0])
        small[2:8, D : D + 256] = jnp.zeros((6, 256), F32)

    dh = dz2_ref[...] + reduce_tokens(
        at, up_back, parts, sc3, rc3, sx3, rx3, fx3, s5, [mlp_weights]
    )
    normed1 = normed_ref[...]
    dz1 = norm_back(dh, normed1, inverse1, gain1)
    dz1_out[...] = dz1
    da = dz1.astype(BF16)
    ag[at.x, at.c] = da
    small[0:1, 0:D] = jnp.sum(dh * normed1, axis=0, keepdims=True)
    small[2:3, 0:D] = jnp.sum(da.astype(F32), axis=0, keepdims=True)
    small[3:4, 0:D] = jnp.sum(dh, axis=0, keepdims=True)
    sends = []

    def out_back(x):
        rows = ag[x].reshape(256, D)
        both = dot_nt(rows[:, 0:256], wr[:, 0, 512:576, :].reshape(128, 256))
        for y in range(1, 4):
            both += dot_nt(rows[:, 256 * y : 256 * y + 256], wr[:, y, 512:576, :].reshape(128, 256))
        both = both.astype(BF16)
        j = len(sends)
        dctx_out[x * 2 + at.z] = pack(both[:, :64])
        dstage[j] = pack(both[:, 64:])
        send = remote(dstage.at[j], dctx_out.at[x * 2 + at.z], ds, j, at.half)
        send.start()
        sends.append(send)

    gather_tokens(at, ag, s6, out_back)
    c2t = c2[...].reshape(1024, 128).T
    for y in range(4):
        cols = slice(256 * y, 256 * y + 256)
        both = dot(c2t, ag[:, :, :, cols].reshape(1024, 256)).astype(BF16)
        grads[0, y, 512:576, :] = both[:64]
        grads[1, y, 512:576, :] = both[64:]
    for send in swaps:
        send.wait_send()
    for send in sends:
        send.wait()


def call(kernel, name, collective, in_places, outs, scratch):
    def spec(place):
        return pl.BlockSpec(memory_space=place)

    return pl.pallas_call(
        kernel,
        out_shape=[jax.ShapeDtypeStruct(out[0], out[1]) for out in outs],
        in_specs=[spec(place) for place in in_places],
        out_specs=[spec(out[2] if len(out) > 2 else VMEM) for out in outs],
        scratch_shapes=scratch,
        compiler_params=pltpu.CompilerParams(
            collective_id=collective, has_side_effects=True, vmem_limit_bytes=56 << 20
        ),
        name=name,
    )


def per_device(
    inputs, w_qkv, b_qv, w_out, w_in, b_in, down_weight, norm_gains, shifts, bias_table, buckets, cotangent
):
    x = inputs[0]
    bucket = jnp.pad(buckets, ((0, 0), (0, 1)), constant_values=BUCKETS)
    xg, wq, wr, packed, probs, context, context_packed = call(
        front_kernel,
        "front",
        0,
        [VMEM] * 9,
        [
            ((4, 2, 128, D), BF16),
            ((2, 4, WQ_ROWS, 256), BF16),
            ((2, 4, WR_ROWS, 256), BF16),
            ((8, 3, 128, 128), BF16),
            ((8, STRIP, LENGTH), BF16, pl.ANY),
            ((LENGTH, 64), F32),
            ((8, 128, 128), BF16),
        ],
        [
            VMEM((4, 3, 128, 128), BF16),
            VMEM((STRIP, BAND), F32),
            VMEM((LENGTH, 64), BF16),
            VMEM((LENGTH, 64), BF16),
            VMEM((8, STRIP, LENGTH), BF16),
            SEMS((2, 10)),
            SEMS((2, 13)),
            SEMS((2, 13)),
            SEMS((2, 4)),
            SEMS((8,)),
        ],
    )(
        x, w_qkv[0].reshape(256, 192), b_qv[0], w_out[0], w_in[0], down_weight[0], b_in, bias_table[0], bucket
    )
    vectors = jnp.concatenate([norm_gains[0], shifts[0], jnp.zeros((2, D), BF16)], axis=0).astype(F32)
    y, dz1, dctx, grads_r, small = call(
        middle_kernel,
        "middle",
        1,
        [VMEM] * 5,
        [
            ((128, D), BF16),
            ((128, D), F32),
            ((8, 128, 128), BF16),
            ((2, 4, 576, 256), BF16),
            ((8, D + 256), F32),
        ],
        [
            VMEM((4, 128, 128), BF16),
            VMEM((4, 2, 128, 128), BF16),
            VMEM((4, 2, 128, D), BF16),
            VMEM((4, 2, 128, D), BF16),
            VMEM((4, 2, 128, D), BF16),
            VMEM((4, 2, 256, 256), BF16),
            VMEM((4, 2, 256, 256), F32),
            VMEM((4, 2, 256, 256), BF16),
            VMEM((4, 2, 128, D), F32),
            *[*REDUCE_SCRATCH] * 3,
            VMEM((128, D), F32),
            VMEM((128, D), F32),
            VMEM((4, 128, 128), BF16),
            SEMS((2, 4)),
            *[SEMS((2, 10))] * 6,
            SEMS((2, 4)),
        ],
    )(context_packed, x, cotangent[0], wr, vectors)
    dx, g_in, g_back, g_out, g_qkv, small_sum, pair, unit, table = call(
        back_kernel,
        "back",
        2,
        [VMEM] * 3 + [pl.ANY] + [VMEM] * 6,
        [
            ((128, D), F32),
            ((256, 256), F32),
            ((256, 256), F32),
            ((64, 256), F32),
            ((256, 192), F32),
            ((8, D), F32),
            ((8, 128), F32),
            ((8, 256), F32),
            ((BUCKETS, 128), F32),
        ],
        [
            VMEM((8, STRIP, LENGTH), BF16),
            VMEM((8, 3, 128, 128), BF16),
            VMEM((4, 3, 128, 128), BF16),
            VMEM((2, 4, 256, 256), BF16),
            VMEM((2, 4, 256, 256), BF16),
            VMEM((4, 2, 128, D), F32),
            VMEM((STRIP, BAND), F32),
            VMEM((LENGTH, 64), BF16),
            VMEM((LENGTH, 64), BF16),
            VMEM((64, LENGTH), F32),
            VMEM((64, LENGTH), F32),
            VMEM((8, STRIP, 64), BF16),
            VMEM((2, 8, D), F32),
            VMEM((4, 8, D), F32),
            VMEM((4, 8, D + 256), F32),
            VMEM((4, 8, D + 256), F32),
            VMEM((4, 40, 128), F32),
            VMEM((2, 40, 128), F32),
            *REDUCE_SCRATCH,
            *reduce_rows_scratch(576),
            *reduce_rows_scratch(256),
            SEMS((8,)),
            SEMS((2, 8)),
            SEMS((2, 10)),
            SEMS((2, 1)),
            *[SEMS((2, 3))] * 4,
            SEMS((2, 1)),
        ],
    )(packed, context, dctx, probs, xg, wq, dz1, grads_r, small, bucket)
    return (
        y[None],
        dx[None],
        g_qkv.reshape(1, 256, 3, 64),
        pair[0].reshape(1, 2, 64),
        g_out[None],
        g_in[None],
        unit[0:1],
        g_back[None],
        small_sum[None, 0:2],
        small_sum[None, 2:6],
        table[None, :, 0:1],
    )


def solution(mesh):
    tokens = P(("replica", "fsdp"), "mp", None)
    qkv, outer, up, down = P(None, "fsdp", None, "mp"), P(None, "mp", "fsdp"), P(None, "fsdp", "mp"), P(None, "mp", "fsdp")
    return jax.shard_map(
        per_device,
        mesh=mesh,
        in_specs=(
            tokens, qkv, P(None, None, "mp"), outer, up, P(None, "mp"), down, P(), P(),
            P(None, None, "mp"), P(("replica", "fsdp"), None), tokens,
        ),
        out_specs=(
            tokens, tokens, qkv, P(None, None, "mp"), outer, up, P(None, "mp"), down, P(), P(), P(None, None, "mp"),
        ),
        check_vma=False,
    )
```
